128 devices in a mesh: dp: 2 (over y_lo), pipe: 16 (over y_hi, z, core), tensor: 4 (over x).
Axes of the slice: x: 4, y: 4 (y_hi: 2, y_lo: 2; y = y_hi * 2 + y_lo), z: 4, core: 2. Of those that a mesh axis runs over, the one named last changes fastest.
Arguments:
- tokens: int32 [256], P('dp'), may hold values from 0 to 25135
- targets: int32 [256], P('dp'), may hold values from 0 to 25135
- hidden: bfloat16 [256, 12288], P('dp', 'pipe'), may hold values from -12 to 12
- embed_grad: bfloat16 [256, 12288], P('dp', 'pipe'), may hold values from -6 to 6
- word_matrix: bfloat16 [25136, 12288], P('tensor', 'pipe'), may hold values from -1 to 1
Outputs:
- token_loss: float32 [256], P(('dp', 'pipe'))
- hidden_grad: bfloat16 [256, 12288], P(('dp', 'tensor'), 'pipe')
- word_grad: float32 [25136, 12288], P(('tensor', 'dp'), 'pipe')
The draws below stay inside these ranges and needn't reach their ends.
All inputs are finite; a program needn't handle non-finite values.
Results may differ from the reference program's by a relative error of at most 0.0034.
Values may be sent and summed in bfloat16 or wider, within the bound.
A program may use at most 128 MiB of HBM per device.

```python
import math
import jax
import jax.numpy as jnp
import numpy as np
from jax import lax

D = 12288
VOCAB = 25136
TOKENS = 256


def shared_rows(key):
    normal_draw = jax.random.truncated_normal(jax.random.fold_in(key, 1), -6.0, 6.0, (VOCAB, D), jnp.float32)
    return normal_draw * (3.0 / math.sqrt(D))


def draw_word_matrix(key, part):
    matrix = shared_rows(key)
    return matrix.astype(jnp.bfloat16)


def draw_hidden(key, part):
    key = jax.random.fold_in(key, 12)
    values = jax.random.truncated_normal(key, -6.0, 6.0, (TOKENS, D), jnp.float32)
    return values.astype(jnp.bfloat16)


def plant(values, own_key, smallest, high):
    index_at = [jax.random.randint(jax.random.fold_in(own_key, axis), (), 0, length) for axis, length in enumerate(values.shape)]
    longest = values.shape.index(max(values.shape))
    neighbour = index_at[:longest] + [(index_at[longest] + 1) % values.shape[longest]] + index_at[longest + 1:]
    return values.at[tuple(index_at)].set(smallest).at[tuple(neighbour)].set(high)


def shard_levels(key, extent, pieces, least, top_value):
    def one(position, blocks):
        steps = jax.random.uniform(jax.random.fold_in(jax.random.fold_in(key, 6), position), (blocks,), jnp.float32, least / len(pieces), top_value / len(pieces))
        return jnp.repeat(jnp.exp(steps), extent[position] // blocks).reshape((-1,) + (1,) * (len(extent) - position - 1))

    factor_of = one(*pieces[0])
    for cut in pieces[1:]:
        factor_of = factor_of * one(*cut)
    return factor_of


def rank_bounds(amount, skew):
    loads = [(1 << 20) // math.isqrt(rank ** skew) + 1 for rank in range(1, amount + 1)]
    deviation = 1 + sum(loads) // (1 << 30)
    return np.cumsum(np.array([max(1, weight // deviation) for weight in loads]))


def ranked(stream_key, shape, number_of, lean):
    grid = rank_bounds(number_of, lean)
    lot = jax.random.randint(jax.random.fold_in(stream_key, 1), shape, 0, int(grid[number_of - 1]))
    rank = jnp.searchsorted(jnp.asarray(grid, jnp.int32), lot, side="right")
    return jax.random.permutation(jax.random.fold_in(stream_key, 2), number_of)[rank].astype(jnp.int32)


def normal_values(stream_key, extent, spread, limit, pieces=(), dtype=jnp.bfloat16):
    entries = jax.random.normal(stream_key, extent, jnp.float32) * spread
    if len(pieces) > 0:
        entries = shard_levels(stream_key, extent, pieces, -0.22, 0.18) * entries
    return jnp.clip(entries, min=-limit, max=limit).astype(dtype)


def setup_inputs(seed: int = 0) -> dict:
    key_list = jax.random.split(jax.random.key(seed), 6)
    tokens = plant(ranked(key_list[0], (TOKENS,), VOCAB, 2), jax.random.fold_in(key_list[0], 3), 0, VOCAB - 1).astype(jnp.int32)
    targets = plant(ranked(key_list[1], (TOKENS,), VOCAB, 1), jax.random.fold_in(key_list[1], 3), 0, VOCAB - 1).astype(jnp.int32)
    hidden = draw_hidden(jax.random.fold_in(key_list[5], 71), 0)
    embed_grad = normal_values(key_list[3], (TOKENS, D), 1.0, 6.0, ((0, 2), (1, 16)))
    word_matrix = draw_word_matrix(jax.random.fold_in(key_list[5], 71), 0)
    return dict(tokens=tokens, targets=targets, hidden=hidden, embed_grad=embed_grad, word_matrix=word_matrix)


def reference(tokens, targets, hidden, embed_grad, word_matrix):
    logits = jnp.dot(hidden, word_matrix.T, preferred_element_type=jnp.float32)
    row_max = jnp.max(logits, axis=1)
    shifted = jnp.exp(logits - row_max[:, None])
    row_total = jnp.sum(shifted, axis=1)
    columns = lax.broadcasted_iota(jnp.int32, logits.shape, 1)
    chosen = columns == targets[:, None]
    target_logit = jnp.sum(jnp.where(chosen, logits, jnp.float32(0.0)), axis=1)
    token_loss = jnp.log(row_total) + row_max - target_logit
    logit_grad = (shifted / row_total[:, None] - chosen.astype(jnp.float32)).astype(jnp.bfloat16)
    hidden_grad = jnp.dot(logit_grad, word_matrix, preferred_element_type=jnp.float32).astype(jnp.bfloat16)
    head_part = jnp.dot(logit_grad.T, hidden, preferred_element_type=jnp.float32)
    lookup = jnp.zeros((VOCAB, D), jnp.float32).at[tokens].add(embed_grad.astype(jnp.float32))
    word_grad = head_part + lookup
    return (token_loss, hidden_grad, word_grad)
```

```python
import functools

import jax
import jax.numpy as jnp
from jax import lax
from jax.experimental import pallas as pl
from jax.experimental.pallas import tpu as pltpu
from jax.sharding import PartitionSpec as P

MESH = pl.DeviceIdType.MESH
BF16, F32, I32, I16 = jnp.bfloat16, jnp.float32, jnp.int32, jnp.int16

DM = 768
VS = 6284
VH = 3142
SH = 6
MAIN = 3136
NC = 3200
CH = 640
NJ = NC // CH
SR = 320
NS = 2 * NJ
TOP = 32767.0


class Place:
    def __init__(self):
        self.d = lax.axis_index("dp")
        self.p = lax.axis_index("pipe")
        self.t = lax.axis_index("tensor")
        self.c = self.p % 2
        self.k = self.p // 2
        self.y = self.k // 4
        self.z = self.k % 4

    def chip(self, k):
        return {"pipe": k * 2 + self.c}

    def partner(self):
        return {"pipe": self.k * 2 + (1 - self.c)}

    def group(self, g):
        return {"dp": g // 4, "tensor": g % 4}


def token_block(k, c):
    y, z = k // 4, k % 4
    return (z % 2) * 8 + (y * 2 + z // 2) * 2 + c


def quantize(x):
    top = jnp.maximum(jnp.max(jnp.abs(x), axis=-1, keepdims=True), 1e-30)
    return jnp.round(x * (TOP / top)).astype(I32).astype(I16), top


def comm_kernel(
    tok_ref, tgt_ref, hid_hbm, emb_hbm, w_hbm, tail0_ref, tail1_ref,
    g_out, hid_out, emb_out, tok_out, loss_out, hg_out,
    wwin, wsh, hid, part, xch, qbuf, scl, rs, rs_scl, tokx, tgtx, lbuf, stat, gbuf,
    hgf, hq, hs, hr, hr_scl,
    w_sem, hid_sem, px_send, px_recv, xc_send, xc_recv, rs_send, rs_recv, sc_send, sc_recv,
    st_send, st_recv, ag_send, ag_recv, pf_send, pf_recv, hg_send, hg_recv, hs_send, hs_recv,
    out_sem,
):
    me = Place()
    d, c, k = me.d, me.c, me.k
    g_me = d * 4 + me.t

    def remote(src, dst, ssem, rsem, to):
        return pltpu.make_async_remote_copy(
            src_ref=src, dst_ref=dst, send_sem=ssem, recv_sem=rsem, device_id=to, device_id_type=MESH
        )

    def w_copy(j):
        rows = CH if j < NJ - 1 else MAIN - (NJ - 1) * CH
        start = pl.multiple_of(d * MAIN + j * CH, 16)
        return pltpu.make_async_copy(
            w_hbm.at[pl.ds(start, rows)], wwin.at[pl.ds(j * CH, rows)], w_sem.at[j]
        )

    own_hid = pltpu.make_async_copy(hid_hbm, hid.at[d], hid_sem)
    own_hid.start()
    for j in range(NJ):
        w_copy(j).start()
    own_emb = pltpu.make_async_copy(emb_hbm, emb_out.at[d], out_sem.at[0])
    own_emb.start()

    bar = pltpu.get_barrier_semaphore()
    pl.semaphore_signal(bar, inc=1, device_id=me.partner(), device_id_type=MESH)
    for o in range(1, 8):
        pl.semaphore_signal(bar, inc=1, device_id=me.chip((k + o) % 8), device_id_type=MESH)
        pl.semaphore_signal(bar, inc=1, device_id=me.group((g_me + o) % 8), device_id_type=MESH)
    pl.semaphore_wait(bar, 15)

    other = {"dp": 1 - d}
    give_hid = remote(hid_hbm, hid.at[d], px_send.at[0], px_recv.at[0], other)
    give_hid.start()
    give_tgt = remote(tgt_ref, tgtx, px_send.at[1], px_recv.at[1], other)
    give_tgt.start()
    give_tok = remote(tok_ref, tokx, px_send.at[2], px_recv.at[2], other)
    give_tok.start()

    row16 = lax.broadcasted_iota(I32, (16, DM), 0)
    tail0 = tail0_ref[...].astype(F32)
    tail1 = jnp.where(row16 < VS - 2 * MAIN, tail1_ref[...].astype(F32), 0.0)
    wwin[pl.ds(MAIN, 16), :] = jnp.where(d == 0, tail0, tail1).astype(BF16)
    wwin[pl.ds(MAIN + 16, NC - MAIN), :] = jnp.zeros((NC - MAIN, DM), BF16)
    scl[...] = jnp.zeros_like(scl)

    def xc_copy(s):
        return remote(part.at[s, :, 1 - c], xch.at[s], xc_send.at[s], xc_recv.at[s], me.partner())

    def target_chip(i, s):
        ph = jnp.where(s < NJ, d, 1 - d)
        return (i // 2) * 4 + 2 * (i % 2) + ph

    def rs_copy(i, s):
        return remote(
            qbuf.at[s, i], rs.at[k, s % NJ], rs_send.at[s, i], rs_recv.at[k, s % NJ],
            me.chip(target_chip(i, s)),
        )

    def sc_copy(i, h):
        return remote(
            scl.at[h, i], rs_scl.at[k], sc_send.at[h, i], sc_recv.at[k], me.chip(target_chip(i, h * NJ))
        )

    def multiply(s):
        j = s % NJ
        who = jnp.where(s < NJ, d, 1 - d)
        cols = pl.ds(pl.multiple_of(j * CH, CH), CH)
        prod = lax.dot_general(
            hid[who], wwin[cols, :], (((1,), (1,)), ((), ())), preferred_element_type=F32
        )
        part[s] = prod.reshape(4, 2, 16, CH)
        xc_copy(s).start()

    def finish(s):
        j = s % NJ
        h = s // NJ
        xc_copy(s).wait_recv()
        total = part[s, :, c] + xch[s]
        code, top = quantize(total)
        qbuf[s] = code
        lane = lax.broadcasted_iota(I32, (4, 16, 128), 2)
        scl[h] = jnp.where(lane == j, top, scl[h])
        for i in range(4):
            to = target_chip(i, s)

            @pl.when(to != k)
            def _():
                rs_copy(i, s).start()

            @pl.when(to == k)
            def _():
                rs[k, j] = qbuf[s, i]

            @pl.when(jnp.logical_and(to != k, j == NJ - 1))
            def _():
                sc_copy(i, h).start()

            @pl.when(jnp.logical_and(to == k, j == NJ - 1))
            def _():
                rs_scl[k] = scl[h, i]

    own_hid.wait()

    def step(s, carry):
        for j in range(NJ):

            @pl.when(s == j)
            def _():
                w_copy(j).wait()

        @pl.when(s == NJ)
        def _():
            give_hid.wait_recv()

        multiply(s)

        @pl.when(s > 0)
        def _():
            finish(s - 1)

        return carry

    lax.fori_loop(0, NS, step, 0)
    finish(NS - 1)

    give_emb = remote(emb_hbm, emb_out.at[d], px_send.at[3], px_recv.at[3], other)
    give_emb.start()
    hid_copy = pltpu.make_async_copy(hid, hid_out, out_sem.at[1])
    hid_copy.start()

    def shift(i, carry):
        rows = pl.multiple_of(i * SR, 64)
        wide = wwin[pl.ds(rows, SR + 16), :].astype(F32)
        moved = jnp.where(d == 0, wide[0:SR, :], wide[SH : SH + SR, :])
        wsh[pl.ds(rows, SR), :] = moved.astype(BF16)
        return carry

    lax.fori_loop(0, NC // SR, shift, 0)
    row_l = lax.broadcasted_iota(I32, (NC - MAIN, DM), 0) + MAIN
    end = wsh[pl.ds(MAIN, NC - MAIN), :].astype(F32)
    wsh[pl.ds(MAIN, NC - MAIN), :] = jnp.where(row_l < VH, end, 0.0).astype(BF16)

    give_tgt.wait_recv()
    give_tok.wait_recv()
    block = token_block(k, c)
    mine = (block // 8) == d
    tgt_row = jnp.where(mine, tgt_ref[...], tgtx[...]).astype(F32)
    lane16 = lax.broadcasted_iota(I32, (16, 128), 1)
    sub16 = lax.broadcasted_iota(I32, (16, 128), 0)
    tgt = jnp.sum(
        jnp.where(lane16 == sub16 + (block % 8) * 16, tgt_row, 0.0), axis=1, keepdims=True
    ).astype(I32)
    offset = me.t * VS + d * VH
    tok_d, tok_o = tok_ref[...], tokx[...]
    sub8 = lax.broadcasted_iota(I32, (8, 128), 0)
    tok_out[...] = jnp.where(sub8 == d, tok_d, tok_o)

    for q in range(8):

        @pl.when(q != k)
        def _():
            for j in range(NJ):
                remote(
                    qbuf.at[0, 0], rs.at[q, j], rs_send.at[0, 0], rs_recv.at[q, j], me.chip(q)
                ).wait_recv()
            remote(
                scl.at[0, 0], rs_scl.at[q], sc_send.at[0, 0], sc_recv.at[q], me.chip(q)
            ).wait_recv()

    for j in range(NJ):
        total = jnp.zeros((16, CH), F32)
        for q in range(8):
            unit = rs_scl[q][:, j : j + 1] * (1.0 / TOP)
            total += rs[q, j].astype(I32).astype(F32) * unit
        lbuf[:, j * CH : (j + 1) * CH] = total

    logits = pltpu.roll(lbuf[...], (NC - SH * d) % NC, 1)
    col = lax.broadcasted_iota(I32, (16, NC), 1)
    valid = col < VH
    logits = jnp.where(valid, logits, -1e30)
    chosen = col == (tgt - offset)
    chosen = jnp.logical_and(chosen, valid)
    m_loc = jnp.max(logits, axis=1, keepdims=True)
    e = jnp.where(valid, jnp.exp(logits - m_loc), 0.0)
    s_loc = jnp.sum(e, axis=1, keepdims=True)
    t_loc = jnp.sum(jnp.where(chosen, logits, 0.0), axis=1, keepdims=True)
    stat[g_me] = jnp.where(lane16 == 0, m_loc, jnp.where(lane16 == 1, s_loc, t_loc))

    def st_copy(o):
        return remote(
            stat.at[g_me], stat.at[g_me], st_send.at[o], st_recv.at[g_me], me.group((g_me + o) % 8)
        )

    for o in range(1, 8):
        st_copy(o).start()
    for o in range(1, 8):
        q = (g_me + o) % 8
        remote(stat.at[g_me], stat.at[q], st_send.at[o], st_recv.at[q], me.group(q)).wait_recv()
    row_max = stat[0][:, 0:1]
    for q in range(1, 8):
        row_max = jnp.maximum(row_max, stat[q][:, 0:1])
    row_total = jnp.zeros((16, 1), F32)
    target_logit = jnp.zeros((16, 1), F32)
    for q in range(8):
        row_total += stat[q][:, 1:2] * jnp.exp(stat[q][:, 0:1] - row_max)
        target_logit += stat[q][:, 2:3]
    loss = jnp.log(row_total) + row_max - target_logit
    grad = e * (jnp.exp(m_loc - row_max) / row_total) - jnp.where(chosen, 1.0, 0.0)
    hi = loss.astype(BF16).astype(F32)
    mid = (loss - hi).astype(BF16).astype(F32)
    low = loss - hi - mid
    grad = jnp.where(col == VH, hi, grad)
    grad = jnp.where(col == VH + 1, mid, grad)
    grad = jnp.where(col == VH + 2, low, grad)

    def rows_of(b):
        return pl.ds(pl.multiple_of(b * 16, 16), 16)

    gbuf[rows_of(block), :] = grad.astype(BF16)

    def ag_copy(o, source):
        rows = rows_of(token_block(source, c))
        return remote(
            gbuf.at[rows], gbuf.at[rows], ag_send.at[o], ag_recv.at[source], me.chip((k + o) % 8)
        )

    def pf_copy(source, core):
        rows = rows_of(token_block(source, core))
        return remote(
            gbuf.at[rows], gbuf.at[rows], pf_send.at[source], pf_recv.at[source], me.partner()
        )

    for o in range(1, 8):
        ag_copy(o, k).start()
    pf_copy(k, c).start()
    for o in range(1, 8):
        source = (k + o) % 8
        ag_copy(o, source).wait_recv()
        pf_copy(source, c).start()
    for q in range(8):
        pf_copy(q, 1 - c).wait_recv()

    g_copy = pltpu.make_async_copy(gbuf, g_out, out_sem.at[2])
    g_copy.start()

    def columns(n, carry):
        cols = pl.ds(pl.multiple_of(n * 256, 256), 256)
        hgf[:, cols] = jnp.dot(gbuf[...], wsh[:, cols], preferred_element_type=F32)
        return carry

    lax.fori_loop(0, DM // 256, columns, 0)
    for g in range(8):
        code, top = quantize(hgf[pl.ds(g * 32, 32), :])
        hq[g] = code
        hs[g] = jnp.broadcast_to(top, (32, 128))

    def hg_copy(o):
        q = (g_me + o) % 8
        return remote(hq.at[q], hr.at[g_me], hg_send.at[o], hg_recv.at[g_me], me.group(q))

    def hs_copy(o):
        q = (g_me + o) % 8
        return remote(hs.at[q], hr_scl.at[g_me], hs_send.at[o], hs_recv.at[g_me], me.group(q))

    for o in range(1, 8):
        hg_copy(o).start()
        hs_copy(o).start()
    hr[g_me] = hq[g_me]
    hr_scl[g_me] = hs[g_me]

    tile = gbuf[rows_of(d * 8 + me.p // 2), pl.ds(NC - 128, 128)].astype(F32)
    half = jnp.where(me.p % 2 == 0, tile[0:8, :], tile[8:16, :])
    lane8 = lax.broadcasted_iota(I32, (8, 128), 1) + (NC - 128)
    here = jnp.logical_and(lane8 >= VH, lane8 < VH + 3)
    value = jnp.sum(jnp.where(here, half, 0.0), axis=1, keepdims=True)
    loss_out[...] = jnp.broadcast_to(value, (8, 128))

    for o in range(1, 8):
        q = (g_me + o) % 8
        remote(hq.at[q], hr.at[q], hg_send.at[o], hg_recv.at[q], me.group(q)).wait_recv()
        remote(hs.at[q], hr_scl.at[q], hs_send.at[o], hs_recv.at[q], me.group(q)).wait_recv()
    total = jnp.zeros((32, DM), F32)
    for q in range(8):
        total += hr[q].astype(I32).astype(F32) * (hr_scl[q][:, 0:1] * (1.0 / TOP))
    hg_out[...] = total.astype(BF16)

    give_hid.wait_send()
    give_tgt.wait_send()
    give_tok.wait_send()
    give_emb.wait()
    own_emb.wait()
    hid_copy.wait()
    g_copy.wait()

    def drain(s, carry):
        xc_copy(s).wait_send()
        for i in range(4):

            @pl.when(target_chip(i, s) != k)
            def _():
                rs_copy(i, s).wait_send()

        return carry

    lax.fori_loop(0, NS, drain, 0)
    for h in range(2):
        for i in range(4):

            @pl.when(target_chip(i, h * NJ) != k)
            def _():
                sc_copy(i, h).wait_send()

    for o in range(1, 8):
        st_copy(o).wait_send()
        ag_copy(o, k).wait_send()
        hg_copy(o).wait_send()
        hs_copy(o).wait_send()
    for q in range(8):
        pf_copy(q, c).wait_send()


def comm_call(tokens, targets, hidden, embed, word):
    any_, vmem = pl.BlockSpec(memory_space=pl.ANY), pl.BlockSpec(memory_space=pltpu.VMEM)
    dma = pltpu.SemaphoreType.DMA
    rows_block = MAIN // 16
    return pl.pallas_call(
        comm_kernel,
        grid=(1,),
        out_shape=(
            jax.ShapeDtypeStruct((256, NC), BF16),
            jax.ShapeDtypeStruct((2, 128, DM), BF16),
            jax.ShapeDtypeStruct((2, 128, DM), BF16),
            jax.ShapeDtypeStruct((8, 128), I32),
            jax.ShapeDtypeStruct((8, 128), F32),
            jax.ShapeDtypeStruct((32, DM), BF16),
        ),
        in_specs=[
            vmem, vmem, any_, any_, any_,
            pl.BlockSpec((16, DM), lambda i: (rows_block, 0)),
            pl.BlockSpec((16, DM), lambda i: (2 * rows_block, 0)),
        ],
        out_specs=(any_, any_, any_, vmem, vmem, vmem),
        scratch_shapes=[
            pltpu.VMEM((NC + 16, DM), BF16),
            pltpu.VMEM((NC, DM), BF16),
            pltpu.VMEM((2, 128, DM), BF16),
            pltpu.VMEM((NS, 4, 2, 16, CH), F32),
            pltpu.VMEM((NS, 4, 16, CH), F32),
            pltpu.VMEM((NS, 4, 16, CH), I16),
            pltpu.VMEM((2, 4, 16, 128), F32),
            pltpu.VMEM((8, NJ, 16, CH), I16),
            pltpu.VMEM((8, 16, 128), F32),
            pltpu.VMEM((1, 128), I32),
            pltpu.VMEM((1, 128), I32),
            pltpu.VMEM((16, NC), F32),
            pltpu.VMEM((8, 16, 128), F32),
            pltpu.VMEM((256, NC), BF16),
            pltpu.VMEM((256, DM), F32),
            pltpu.VMEM((8, 32, DM), I16),
            pltpu.VMEM((8, 32, 128), F32),
            pltpu.VMEM((8, 32, DM), I16),
            pltpu.VMEM((8, 32, 128), F32),
            dma((NJ,)),
            dma,
            dma((4,)),
            dma((4,)),
            dma((NS,)),
            dma((NS,)),
            dma((NS, 4)),
            dma((8, NJ)),
            dma((2, 4)),
            dma((8,)),
            dma((8,)),
            dma((8,)),
            dma((8,)),
            dma((8,)),
            dma((8,)),
            dma((8,)),
            dma((8,)),
            dma((8,)),
            dma((8,)),
            dma((8,)),
            dma((3,)),
        ],
        compiler_params=pltpu.CompilerParams(
            collective_id=0, has_side_effects=True, vmem_limit_bytes=48 * 2**20
        ),
        name="logit_grad",
    )(tokens, targets, hidden, embed, word, word, word)


RB = 640


def word_kernel(g_ref, hid_ref, emb_ref, tok_ref, loss_ref, hg_ref, out_ref, loss_out, hg_out):
    i = pl.program_id(0)
    base = lax.axis_index("tensor") * VS + lax.axis_index("dp") * VH + i * RB
    rows = lax.broadcasted_iota(I32, (RB, 128), 0) + base
    tok = tok_ref[...]
    hot = jnp.concatenate(
        [jnp.where(rows == tok[h : h + 1, :], 1.0, 0.0).astype(BF16) for h in range(2)], axis=1
    )
    head = lax.dot_general(
        g_ref[...], hid_ref[...], (((0,), (0,)), ((), ())), preferred_element_type=F32
    )
    out_ref[...] = head + jnp.dot(hot, emb_ref[...], preferred_element_type=F32)

    @pl.when(i == 0)
    def _():
        sub = lax.broadcasted_iota(I32, (8, 128), 0)
        lane = lax.broadcasted_iota(I32, (8, 128), 1)
        row = jnp.sum(jnp.where(sub == lane, loss_ref[...], 0.0), axis=0, keepdims=True)
        loss_out[...] = row[:, 0:8]
        hg_out[...] = hg_ref[...]


def word_call(grad, hid, emb, tok, loss, hg):
    def whole(*shape):
        return pl.BlockSpec(shape, lambda i: (0,) * len(shape))

    return pl.pallas_call(
        word_kernel,
        grid=(pl.cdiv(VH, RB),),
        out_shape=(
            jax.ShapeDtypeStruct((VH, DM), F32),
            jax.ShapeDtypeStruct((1, 8), F32),
            jax.ShapeDtypeStruct((32, DM), BF16),
        ),
        in_specs=[
            pl.BlockSpec((256, RB), lambda i: (0, i)),
            whole(256, DM), whole(256, DM), whole(8, 128), whole(8, 128), whole(32, DM),
        ],
        out_specs=(pl.BlockSpec((RB, DM), lambda i: (i, 0)), whole(1, 8), whole(32, DM)),
        compiler_params=pltpu.CompilerParams(vmem_limit_bytes=48 * 2**20),
        name="word_grad",
    )(grad, hid, emb, tok, loss, hg)


def local(tokens, targets, hidden, embed_grad, word_matrix):
    grad, hid, emb, tok, loss, hg = comm_call(
        tokens.reshape(1, 128), targets.reshape(1, 128), hidden, embed_grad, word_matrix
    )
    word, loss, hg = word_call(
        grad, hid.reshape(256, DM), emb.reshape(256, DM), tok, loss, hg
    )
    return loss.reshape(8), hg, word


def solution(mesh):
    return jax.shard_map(
        local,
        mesh=mesh,
        in_specs=(P("dp"), P("dp"), P("dp", "pipe"), P("dp", "pipe"), P("tensor", "pipe")),
        out_specs=(P(("dp", "pipe")), P(("dp", "tensor"), "pipe"), P(("tensor", "dp"), "pipe")),
        check_vma=False,
    )
```

```python
import functools

import jax
import jax.numpy as jnp
from jax import lax
from jax.experimental import pallas as pl
from jax.experimental.pallas import tpu as pltpu
from jax.sharding import PartitionSpec as P

MESH = pl.DeviceIdType.MESH
BF16, F32, I32, I16 = jnp.bfloat16, jnp.float32, jnp.int32, jnp.int16

DM = 768
VS = 6284
VH = 3142
SH = 6
MAIN = 3136
NC = 3200
CH = 640
NJ = NC // CH
ENDS = (0, 2, 4, NJ)
NP = len(ENDS) - 1
AHEAD = 2
NQ = NC + 128
LAG = 2
HN = 256
SR = 320
NS = 2 * NJ
TOP = 32767.0


class Place:
    def __init__(self):
        self.d = lax.axis_index("dp")
        self.p = lax.axis_index("pipe")
        self.t = lax.axis_index("tensor")
        self.c = self.p % 2
        self.k = self.p // 2

    def chip(self, k):
        return {"pipe": k * 2 + self.c}

    def partner(self):
        return {"pipe": self.k * 2 + (1 - self.c)}

    def group(self, g):
        return {"dp": g // 4, "tensor": g % 4}

    def row_group(self, g):
        return {"tensor": g // 2, "pipe": self.k * 2 + g % 2}

    def half_group(self, q):
        return {"dp": self.c, "pipe": q * 2 + self.d}


LN2_16 = 0.6931471805599453 / 16


def scale_of(code):
    return jnp.exp(code * LN2_16)


def quantize(x):
    top = jnp.maximum(jnp.max(jnp.abs(x), axis=-1, keepdims=True), 1e-30)
    code = jnp.ceil(jnp.log(top) * (1 / LN2_16) + 0.1)
    return jnp.round(x * (TOP / scale_of(code))).astype(I32).astype(I16), code


def comm_kernel(
    tok_ref, tgt_ref, hid_hbm, emb_hbm, w_hbm, tail_ref,
    g_out, hid_out, emb_out, tok_out, loss_out, hg_out,
    wwin, wsh, hid, emb, part, xch, qbuf, rs, tokx, lbuf, stat, gsend, gbuf,
    hgf, hq, hr,
    w_sem, hid_sem, px_send, px_recv, xc_send, xc_recv, rs_send, rs_recv,
    st_send, st_recv, ag_send, ag_recv, pf_send, pf_recv, hg_send, hg_recv,
    out_sem,
):
    me = Place()
    d, c, k = me.d, me.c, me.k
    h = c
    g_me = d * 4 + me.t
    r_me = me.t * 2 + h

    def remote(src, dst, ssem, rsem, to):
        return pltpu.make_async_remote_copy(
            src_ref=src, dst_ref=dst, send_sem=ssem, recv_sem=rsem, device_id=to, device_id_type=MESH
        )

    def w_copy(v, j):
        rows = CH if j < NJ - 1 else MAIN - (NJ - 1) * CH + (16 if v == 0 else 0)
        return pltpu.make_async_copy(
            w_hbm.at[pl.ds(v * MAIN + j * CH, rows)],
            wwin.at[v, pl.ds(j * CH, rows)],
            w_sem.at[v, j],
        )

    own_hid = pltpu.make_async_copy(hid_hbm, hid.at[d], hid_sem.at[0])
    own_hid.start()
    for j in range(AHEAD):
        for v in range(2):
            w_copy(v, j).start()
    own_emb = pltpu.make_async_copy(emb_hbm, emb.at[d], hid_sem.at[1])
    own_emb.start()

    bar = pltpu.get_barrier_semaphore()

    def greet(to):
        pl.semaphore_signal(bar, inc=1, device_id=to, device_id_type=MESH)

    greet(me.partner())
    for o in range(1, 8):
        greet(me.chip((k + o) % 8))
        greet(me.group((g_me + o) % 8))
    for o in range(1, 4):
        greet({"tensor": (me.t + o) % 4, "pipe": k * 2 + 1 - c})

    for q in range(8):
        greet({"dp": 1 - d, "pipe": q * 2 + 1 - c})
    pl.semaphore_wait(bar, 26)

    other = {"dp": 1 - d}
    give_hid = remote(hid.at[d], hid.at[d], px_send.at[0], px_recv.at[0], other)
    give_tok = remote(tok_ref, tokx, px_send.at[2], px_recv.at[2], other)
    give_tok.start()

    row16 = lax.broadcasted_iota(I32, (16, DM), 0)
    tail = jnp.where(row16 < VS - 2 * MAIN, tail_ref[...].astype(F32), 0.0)
    wwin[1, pl.ds(MAIN, 16), :] = tail.astype(BF16)
    for v in range(2):
        wwin[v, pl.ds(MAIN + 16, NC - MAIN), :] = jnp.zeros((NC - MAIN, DM), BF16)
    qbuf[:, :, pl.ds(NC, 128)] = jnp.zeros((8, 16, 128), I16)

    def xc_copy(s):
        return remote(part.at[s], xch.at[s // 2], xc_send.at[s // 2], xc_recv.at[s // 2], me.partner())

    def rs_copy(q, part_no, source):
        first, end = ENDS[part_no] * CH, ENDS[part_no + 1] * CH
        cols = pl.ds(first, (end if part_no < NP - 1 else NQ) - first)
        return remote(
            qbuf.at[q, :, cols], rs.at[source, :, cols], rs_send.at[part_no, q],
            rs_recv.at[part_no, source], me.chip(q),
        )

    def multiply(s):
        v = s % 2
        cols = pl.ds(pl.multiple_of((s // 2) * CH, CH), CH)
        prod = lax.dot_general(
            hid[d], wwin[v, cols, :], (((1,), (1,)), ((), ())), preferred_element_type=F32
        )
        part[s] = prod.reshape(8, 16, CH)

    def finish(j):
        xc_copy(2 * j + c).wait_recv()
        total = part[2 * j + c] + xch[j]
        code, scale = quantize(total)
        qbuf[:, :, pl.ds(pl.multiple_of(j * CH, CH), CH)] = code
        lane = lax.broadcasted_iota(I32, (8, 16, 128), 2)
        kept = qbuf[:, :, pl.ds(NC, 128)].astype(I32)
        kept = jnp.where(lane == j, scale.astype(I32), kept)
        qbuf[:, :, pl.ds(NC, 128)] = kept.astype(I16)
        for part_no in range(NP):

            @pl.when(j == ENDS[part_no + 1] - 1)
            def _():
                for o in range(1, 8):
                    rs_copy((k + o) % 8, part_no, k).start()

    own_hid.wait()
    give_hid.start()

    def step(j, carry):
        for jj in range(NJ):

            @pl.when(j == jj)
            def _():
                w_copy(0, jj).wait()
                w_copy(1, jj).wait()
                if jj + AHEAD < NJ:
                    w_copy(0, jj + AHEAD).start()
                    w_copy(1, jj + AHEAD).start()

        multiply(2 * j + 1 - c)
        xc_copy(2 * j + 1 - c).start()
        multiply(2 * j + c)

        @pl.when(j >= LAG)
        def _():
            finish(j - LAG)

        return carry

    lax.fori_loop(0, NJ, step, 0)

    def finish_step(j, carry):
        finish(j)
        return carry

    lax.fori_loop(NJ - LAG, NJ, finish_step, 0)
    rs[k] = qbuf[k]

    def shift(i, carry):
        rows = pl.multiple_of(i * SR, 64)
        wide = wwin[d, pl.ds(rows, SR + 16), :].astype(F32)
        moved = jnp.where(d == 0, wide[0:SR, :], wide[SH : SH + SR, :])
        wsh[pl.ds(rows, SR), :] = moved.astype(BF16)
        return carry

    lax.fori_loop(0, NC // SR, shift, 0)
    row_l = lax.broadcasted_iota(I32, (NC - MAIN, DM), 0) + MAIN
    end = wsh[pl.ds(MAIN, NC - MAIN), :].astype(F32)
    wsh[pl.ds(MAIN, NC - MAIN), :] = jnp.where(row_l < VH, end, 0.0).astype(BF16)

    lane16 = lax.broadcasted_iota(I32, (16, 128), 1)
    sub16 = lax.broadcasted_iota(I32, (16, 128), 0)
    tgt = jnp.sum(
        jnp.where(lane16 == sub16 + k * 16, tgt_ref[...].astype(F32), 0.0), axis=1, keepdims=True
    ).astype(I32)
    offset = me.t * VS + h * VH
    give_tok.wait_recv()
    sub8 = lax.broadcasted_iota(I32, (8, 128), 0)
    tok_out[...] = jnp.where(sub8 == d, tok_ref[...], tokx[...])

    for o in range(1, 8):
        for part_no in range(NP):
            rs_copy((k + o) % 8, part_no, (k + o) % 8).wait_recv()

    own_emb.wait()
    give_emb = remote(emb.at[d], emb.at[d], px_send.at[3], px_recv.at[3], other)
    give_emb.start()

    units = [scale_of(rs[q, :, NC:NQ].astype(I32).astype(F32)) * (1.0 / TOP) for q in range(8)]
    for j in range(NJ):
        total = jnp.zeros((16, CH), F32)
        for q in range(8):
            total += rs[q, :, j * CH : (j + 1) * CH].astype(I32).astype(F32) * units[q][:, j : j + 1]
        lbuf[:, j * CH : (j + 1) * CH] = total

    logits = pltpu.roll(lbuf[...], (NC - SH * h) % NC, 1)
    col = lax.broadcasted_iota(I32, (16, NC), 1)
    valid = col < VH
    logits = jnp.where(valid, logits, -1e30)
    chosen = jnp.logical_and(col == (tgt - offset), valid)
    m_loc = jnp.max(logits, axis=1, keepdims=True)
    e = jnp.where(valid, jnp.exp(logits - m_loc), 0.0)
    s_loc = jnp.sum(e, axis=1, keepdims=True)
    t_loc = jnp.sum(jnp.where(chosen, logits, 0.0), axis=1, keepdims=True)
    stat[r_me] = jnp.where(lane16 == 0, m_loc, jnp.where(lane16 == 1, s_loc, t_loc))

    def st_copy(o):
        return remote(
            stat.at[r_me], stat.at[r_me], st_send.at[o], st_recv.at[r_me], me.row_group((r_me + o) % 8)
        )

    for o in range(1, 8):
        st_copy(o).start()
    for o in range(1, 8):
        q = (r_me + o) % 8
        remote(stat.at[r_me], stat.at[q], st_send.at[o], st_recv.at[q], me.row_group(q)).wait_recv()
    row_max = stat[0][:, 0:1]
    for q in range(1, 8):
        row_max = jnp.maximum(row_max, stat[q][:, 0:1])
    row_total = jnp.zeros((16, 1), F32)
    target_logit = jnp.zeros((16, 1), F32)
    for q in range(8):
        row_total += stat[q][:, 1:2] * jnp.exp(stat[q][:, 0:1] - row_max)
        target_logit += stat[q][:, 2:3]
    loss = jnp.log(row_total) + row_max - target_logit
    grad = e * (jnp.exp(m_loc - row_max) / row_total) - jnp.where(chosen, 1.0, 0.0)
    hi = loss.astype(BF16).astype(F32)
    mid = (loss - hi).astype(BF16).astype(F32)
    low = loss - hi - mid
    grad = jnp.where(col == VH, hi, grad)
    grad = jnp.where(col == VH + 1, mid, grad)
    grad = jnp.where(col == VH + 2, low, grad)

    def rows_of(b):
        return pl.ds(pl.multiple_of(b * 16, 16), 16)

    gsend[...] = grad.astype(BF16)

    @pl.when(c == d)
    def _():
        gbuf[rows_of(d * 8 + k), :] = gsend[...]

    def ag_copy(q):
        return remote(
            gsend, gbuf.at[rows_of(d * 8 + k)], ag_send.at[q], ag_recv.at[k], me.half_group(q)
        )

    def pf_copy(u, core):
        rows = rows_of(core * 8 + u)
        return remote(gbuf.at[rows], gbuf.at[rows], pf_send.at[u], pf_recv.at[u], me.partner())

    def is_other(q):
        return jnp.logical_or(c != d, q != k)

    for o in range(8):
        q = (k + o) % 8

        @pl.when(is_other(q))
        def _():
            ag_copy(q).start()

    for o in range(8):
        u = (k + o) % 8

        @pl.when(is_other(u))
        def _():
            remote(
                gsend, gbuf.at[rows_of(c * 8 + u)], ag_send.at[0], ag_recv.at[u], me.partner()
            ).wait_recv()

        pf_copy(u, c).start()
    for u in range(8):
        pf_copy(u, 1 - c).wait_recv()

    g_copy = pltpu.make_async_copy(gbuf, g_out, out_sem.at[2])
    g_copy.start()
    give_hid.wait_recv()
    hid_copy = pltpu.make_async_copy(hid, hid_out, out_sem.at[1])
    hid_copy.start()
    give_emb.wait_recv()
    emb_copy = pltpu.make_async_copy(emb, emb_out, out_sem.at[0])
    emb_copy.start()

    def hg_copy(o):
        q = (g_me + o) % 8
        return remote(hq.at[q], hr.at[g_me], hg_send.at[o], hg_recv.at[g_me], me.group(q))

    def columns(n, carry):
        cols = pl.ds(pl.multiple_of(n * HN, HN), HN)
        hgf[:, cols] = jnp.dot(gbuf[...], wsh[:, cols], preferred_element_type=F32)
        return carry

    lax.fori_loop(0, DM // HN, columns, 0)
    code, scale = quantize(hgf[...].reshape(8, 32, DM))
    hq[:, :, 0:DM] = code
    hq[:, :, DM:] = jnp.broadcast_to(scale, (8, 32, 128)).astype(I32).astype(I16)
    for o in range(1, 8):
        hg_copy(o).start()
    hr[g_me] = hq[g_me]

    tile = gbuf[rows_of(d * 8 + me.p // 2), pl.ds(NC - 128, 128)].astype(F32)
    half = jnp.where(me.p % 2 == 0, tile[0:8, :], tile[8:16, :])
    lane8 = lax.broadcasted_iota(I32, (8, 128), 1)
    here = jnp.logical_and(lane8 >= VH - (NC - 128), lane8 < VH + 3 - (NC - 128))
    value = jnp.sum(jnp.where(here, half, 0.0), axis=1, keepdims=True)
    loss_out[...] = jnp.broadcast_to(value, (8, 128))

    for o in range(1, 8):
        q = (g_me + o) % 8
        remote(hq.at[q], hr.at[q], hg_send.at[o], hg_recv.at[q], me.group(q)).wait_recv()
    total = jnp.zeros((32, DM), F32)
    for q in range(8):
        unit = scale_of(hr[q, :, DM:].astype(I32).astype(F32))[:, 0:1] * (1.0 / TOP)
        total += hr[q, :, 0:DM].astype(I32).astype(F32) * unit
    hg_out[...] = total.astype(BF16)

    give_hid.wait_send()
    give_tok.wait_send()
    give_emb.wait_send()
    emb_copy.wait()
    hid_copy.wait()
    g_copy.wait()

    def drain(j, carry):
        xc_copy(2 * j + 1 - c).wait_send()
        return carry

    lax.fori_loop(0, NJ, drain, 0)
    for o in range(1, 8):
        for part_no in range(NP):
            rs_copy((k + o) % 8, part_no, k).wait_send()
    for o in range(1, 8):
        st_copy(o).wait_send()
    for q in range(8):

        @pl.when(is_other(q))
        def _():
            ag_copy(q).wait_send()

    for q in range(8):
        pf_copy(q, c).wait_send()
    for o in range(1, 8):
        hg_copy(o).wait_send()


def comm_call(tokens, targets, hidden, embed, word):
    any_, vmem = pl.BlockSpec(memory_space=pl.ANY), pl.BlockSpec(memory_space=pltpu.VMEM)
    dma = pltpu.SemaphoreType.DMA
    return pl.pallas_call(
        comm_kernel,
        grid=(1,),
        out_shape=(
            jax.ShapeDtypeStruct((256, NC), BF16),
            jax.ShapeDtypeStruct((2, 128, DM), BF16),
            jax.ShapeDtypeStruct((2, 128, DM), BF16),
            jax.ShapeDtypeStruct((8, 128), I32),
            jax.ShapeDtypeStruct((8, 128), F32),
            jax.ShapeDtypeStruct((32, DM), BF16),
        ),
        in_specs=[
            vmem, vmem, any_, any_, any_,
            pl.BlockSpec((16, DM), lambda i: (2 * MAIN // 16, 0)),
        ],
        out_specs=(any_, any_, any_, vmem, vmem, vmem),
        scratch_shapes=[
            pltpu.VMEM((2, NC + 16, DM), BF16),
            pltpu.VMEM((NC, DM), BF16),
            pltpu.VMEM((2, 128, DM), BF16),
            pltpu.VMEM((2, 128, DM), BF16),
            pltpu.VMEM((NS, 8, 16, CH), F32),
            pltpu.VMEM((NJ, 8, 16, CH), F32),
            pltpu.VMEM((8, 16, NQ), I16),
            pltpu.VMEM((8, 16, NQ), I16),
            pltpu.VMEM((1, 128), I32),
            pltpu.VMEM((16, NC), F32),
            pltpu.VMEM((8, 16, 128), F32),
            pltpu.VMEM((16, NC), BF16),
            pltpu.VMEM((256, NC), BF16),
            pltpu.VMEM((256, DM), F32),
            pltpu.VMEM((8, 32, DM + 128), I16),
            pltpu.VMEM((8, 32, DM + 128), I16),
            dma((2, NJ)),
            dma((2,)),
            dma((4,)),
            dma((4,)),
            dma((NJ,)),
            dma((NJ,)),
            dma((NP, 8)),
            dma((NP, 8)),
            dma((8,)),
            dma((8,)),
            dma((8,)),
            dma((8,)),
            dma((8,)),
            dma((8,)),
            dma((8,)),
            dma((8,)),
            dma((3,)),
        ],
        compiler_params=pltpu.CompilerParams(
            collective_id=0, has_side_effects=True, vmem_limit_bytes=60 * 2**20
        ),
        name="logit_grad",
    )(tokens, targets, hidden, embed, word, word)


RB = 640


def word_kernel(g_ref, hid_ref, emb_ref, tok_ref, loss_ref, hg_ref, out_ref, loss_out, hg_out):
    i = pl.program_id(0)
    base = lax.axis_index("tensor") * VS + lax.axis_index("dp") * VH + i * RB
    rows = lax.broadcasted_iota(I32, (RB, 128), 0) + base
    tok = tok_ref[...]
    hot = jnp.concatenate(
        [jnp.where(rows == tok[h : h + 1, :], 1.0, 0.0).astype(BF16) for h in range(2)], axis=1
    )
    head = lax.dot_general(
        g_ref[...], hid_ref[...], (((0,), (0,)), ((), ())), preferred_element_type=F32
    )
    out_ref[...] = head + jnp.dot(hot, emb_ref[...], preferred_element_type=F32)

    @pl.when(i == 0)
    def _():
        sub = lax.broadcasted_iota(I32, (8, 128), 0)
        lane = lax.broadcasted_iota(I32, (8, 128), 1)
        row = jnp.sum(jnp.where(sub == lane, loss_ref[...], 0.0), axis=0, keepdims=True)
        loss_out[...] = row[:, 0:8]
        hg_out[...] = hg_ref[...]


def word_call(grad, hid, emb, tok, loss, hg):
    def whole(*shape):
        return pl.BlockSpec(shape, lambda i: (0,) * len(shape))

    return pl.pallas_call(
        word_kernel,
        grid=(pl.cdiv(VH, RB),),
        out_shape=(
            jax.ShapeDtypeStruct((VH, DM), F32),
            jax.ShapeDtypeStruct((1, 8), F32),
            jax.ShapeDtypeStruct((32, DM), BF16),
        ),
        in_specs=[
            pl.BlockSpec((256, RB), lambda i: (0, i)),
            whole(256, DM), whole(256, DM), whole(8, 128), whole(8, 128), whole(32, DM),
        ],
        out_specs=(pl.BlockSpec((RB, DM), lambda i: (i, 0)), whole(1, 8), whole(32, DM)),
        compiler_params=pltpu.CompilerParams(vmem_limit_bytes=60 * 2**20),
        name="word_grad",
    )(grad, hid, emb, tok, loss, hg)


def local(tokens, targets, hidden, embed_grad, word_matrix):
    grad, hid, emb, tok, loss, hg = comm_call(
        tokens.reshape(1, 128), targets.reshape(1, 128), hidden, embed_grad, word_matrix
    )
    word, loss, hg = word_call(
        grad, hid.reshape(256, DM), emb.reshape(256, DM), tok, loss, hg
    )
    return loss.reshape(8), hg, word


def solution(mesh):
    return jax.shard_map(
        local,
        mesh=mesh,
        in_specs=(P("dp"), P("dp"), P("dp", "pipe"), P("dp", "pipe"), P("tensor", "pipe")),
        out_specs=(P(("dp", "pipe")), P(("dp", "tensor"), "pipe"), P(("tensor", "dp"), "pipe")),
        check_vma=False,
    )
```

```python
import functools

import jax
import jax.numpy as jnp
from jax import lax
from jax.experimental import pallas as pl
from jax.experimental.pallas import tpu as pltpu
from jax.sharding import PartitionSpec as P

MESH = pl.DeviceIdType.MESH
BF16, F32, I32, I16 = jnp.bfloat16, jnp.float32, jnp.int32, jnp.int16

DM = 768
VS = 6284
VH = 3142
SH = 6
MAIN = 3136
NC = 3200
CH = 640
NJ = NC // CH
ENDS = (0, 2, 4, NJ)
NP = len(ENDS) - 1
AHEAD = 2
NQ = NC + 128
LAG = 2
HN = 256
SR = 320
NS = 2 * NJ
TOP = 32767.0


class Place:
    def __init__(self):
        self.d = lax.axis_index("dp")
        self.p = lax.axis_index("pipe")
        self.t = lax.axis_index("tensor")
        self.c = self.p % 2
        self.k = self.p // 2

    def chip(self, k):
        return {"pipe": k * 2 + self.c}

    def partner(self):
        return {"pipe": self.k * 2 + (1 - self.c)}

    def group(self, g):
        return {"dp": g // 4, "tensor": g % 4}

    def row_group(self, g):
        return {"tensor": g // 2, "pipe": self.k * 2 + g % 2}

    def half_group(self, q):
        return {"dp": self.c, "pipe": q * 2 + self.d}


LN2_16 = 0.6931471805599453 / 16


def scale_of(code):
    return jnp.exp(code * LN2_16)


def quantize(x):
    top = jnp.maximum(jnp.max(jnp.abs(x), axis=-1, keepdims=True), 1e-30)
    code = jnp.ceil(jnp.log(top) * (1 / LN2_16) + 0.1)
    return jnp.round(x * (TOP / scale_of(code))).astype(I32).astype(I16), code


def comm_kernel(
    tok_ref, tgt_ref, hid_hbm, emb_hbm, w_hbm, tail_ref,
    g_out, hid_out, emb_out, tok_out, loss_out, hg_out,
    wwin, wsh, hid, emb, part, xch, qbuf, rs, tokx, lbuf, stat, gsend, gbuf,
    hgf, hq, hr,
    w_sem, hid_sem, px_send, px_recv, xc_send, xc_recv, rs_send, rs_recv,
    st_send, st_recv, ag_send, ag_recv, pf_send, pf_recv, hg_send, hg_recv,
    out_sem,
):
    me = Place()
    d, c, k = me.d, me.c, me.k
    h = c
    g_me = d * 4 + me.t
    r_me = me.t * 2 + h

    def remote(src, dst, ssem, rsem, to):
        return pltpu.make_async_remote_copy(
            src_ref=src, dst_ref=dst, send_sem=ssem, recv_sem=rsem, device_id=to, device_id_type=MESH
        )

    def w_copy(v, j):
        rows = CH if j < NJ - 1 else MAIN - (NJ - 1) * CH + (16 if v == 0 else 0)
        return pltpu.make_async_copy(
            w_hbm.at[pl.ds(v * MAIN + j * CH, rows)],
            wwin.at[v, pl.ds(j * CH, rows)],
            w_sem.at[v, j],
        )

    own_hid = pltpu.make_async_copy(hid_hbm, hid.at[d], hid_sem.at[0])
    own_hid.start()
    for j in range(AHEAD):
        for v in range(2):
            w_copy(v, j).start()
    own_emb = pltpu.make_async_copy(emb_hbm, emb.at[d], hid_sem.at[1])
    own_emb.start()

    bar = pltpu.get_barrier_semaphore()

    def greet(to):
        pl.semaphore_signal(bar, inc=1, device_id=to, device_id_type=MESH)

    greet(me.partner())
    for o in range(1, 8):
        greet(me.chip((k + o) % 8))
        greet(me.group((g_me + o) % 8))
    for o in range(1, 4):
        greet({"tensor": (me.t + o) % 4, "pipe": k * 2 + 1 - c})

    for q in range(8):
        greet({"dp": 1 - d, "pipe": q * 2 + 1 - c})
    pl.semaphore_wait(bar, 26)

    other = {"dp": 1 - d}
    give_hid = remote(hid.at[d], hid.at[d], px_send.at[0], px_recv.at[0], other)
    give_tok = remote(tok_ref, tokx, px_send.at[2], px_recv.at[2], other)
    give_tok.start()

    row16 = lax.broadcasted_iota(I32, (16, DM), 0)
    tail = jnp.where(row16 < VS - 2 * MAIN, tail_ref[...].astype(F32), 0.0)
    wwin[1, pl.ds(MAIN, 16), :] = tail.astype(BF16)
    for v in range(2):
        wwin[v, pl.ds(MAIN + 16, NC - MAIN), :] = jnp.zeros((NC - MAIN, DM), BF16)
    qbuf[:, :, pl.ds(NC, 128)] = jnp.zeros((8, 16, 128), I16)

    def xc_copy(s):
        return remote(part.at[s], xch.at[s // 2], xc_send.at[s // 2], xc_recv.at[s // 2], me.partner())

    def rs_copy(q, part_no, source):
        first, end = ENDS[part_no] * CH, ENDS[part_no + 1] * CH
        cols = pl.ds(first, (end if part_no < NP - 1 else NQ) - first)
        return remote(
            qbuf.at[q, :, cols], rs.at[source, :, cols], rs_send.at[part_no, q],
            rs_recv.at[part_no, source], me.chip(q),
        )

    def multiply(s):
        v = s % 2
        cols = pl.ds(pl.multiple_of((s // 2) * CH, CH), CH)
        prod = lax.dot_general(
            hid[d], wwin[v, cols, :], (((1,), (1,)), ((), ())), preferred_element_type=F32
        )
        part[s] = prod.reshape(8, 16, CH)

    def finish(j):
        xc_copy(2 * j + c).wait_recv()
        total = part[2 * j + c] + xch[j]
        code, scale = quantize(total)
        qbuf[:, :, pl.ds(pl.multiple_of(j * CH, CH), CH)] = code
        lane = lax.broadcasted_iota(I32, (8, 16, 128), 2)
        kept = qbuf[:, :, pl.ds(NC, 128)].astype(I32)
        kept = jnp.where(lane == j, scale.astype(I32), kept)
        qbuf[:, :, pl.ds(NC, 128)] = kept.astype(I16)
        for part_no in range(NP):

            @pl.when(j == ENDS[part_no + 1] - 1)
            def _():
                for o in range(1, 8):
                    rs_copy((k + o) % 8, part_no, k).start()

    own_hid.wait()
    give_hid.start()

    def step(j, carry):
        for jj in range(NJ):

            @pl.when(j == jj)
            def _():
                w_copy(0, jj).wait()
                w_copy(1, jj).wait()
                if jj + AHEAD < NJ:
                    w_copy(0, jj + AHEAD).start()
                    w_copy(1, jj + AHEAD).start()

        multiply(2 * j + 1 - c)
        xc_copy(2 * j + 1 - c).start()
        multiply(2 * j + c)

        @pl.when(j >= LAG)
        def _():
            finish(j - LAG)

        return carry

    lax.fori_loop(0, NJ, step, 0)

    def finish_step(j, carry):
        finish(j)
        return carry

    lax.fori_loop(NJ - LAG, NJ, finish_step, 0)
    rs[k] = qbuf[k]

    def shift(i, carry):
        rows = pl.multiple_of(i * SR, 64)
        wide = wwin[d, pl.ds(rows, SR + 16), :].astype(F32)
        moved = jnp.where(d == 0, wide[0:SR, :], wide[SH : SH + SR, :])
        wsh[pl.ds(rows, SR), :] = moved.astype(BF16)
        return carry

    lax.fori_loop(0, NC // SR, shift, 0)
    row_l = lax.broadcasted_iota(I32, (NC - MAIN, DM), 0) + MAIN
    end = wsh[pl.ds(MAIN, NC - MAIN), :].astype(F32)
    wsh[pl.ds(MAIN, NC - MAIN), :] = jnp.where(row_l < VH, end, 0.0).astype(BF16)

    lane16 = lax.broadcasted_iota(I32, (16, 128), 1)
    sub16 = lax.broadcasted_iota(I32, (16, 128), 0)
    tgt = jnp.sum(
        jnp.where(lane16 == sub16 + k * 16, tgt_ref[...].astype(F32), 0.0), axis=1, keepdims=True
    ).astype(I32)
    offset = me.t * VS + h * VH
    give_tok.wait_recv()
    sub8 = lax.broadcasted_iota(I32, (8, 128), 0)
    tok_out[...] = jnp.where(sub8 == d, tok_ref[...], tokx[...])

    for o in range(1, 8):
        for part_no in range(NP):
            rs_copy((k + o) % 8, part_no, (k + o) % 8).wait_recv()

    own_emb.wait()
    give_emb = remote(emb.at[d], emb.at[d], px_send.at[3], px_recv.at[3], other)
    give_emb.start()

    units = [scale_of(rs[q, :, NC:NQ].astype(I32).astype(F32)) * (1.0 / TOP) for q in range(8)]
    for j in range(NJ):
        total = jnp.zeros((16, CH), F32)
        for q in range(8):
            total += rs[q, :, j * CH : (j + 1) * CH].astype(I32).astype(F32) * units[q][:, j : j + 1]
        lbuf[:, j * CH : (j + 1) * CH] = total

    logits = pltpu.roll(lbuf[...], (NC - SH * h) % NC, 1)
    col = lax.broadcasted_iota(I32, (16, NC), 1)
    valid = col < VH
    logits = jnp.where(valid, logits, -1e30)
    chosen = jnp.logical_and(col == (tgt - offset), valid)
    m_loc = jnp.max(logits, axis=1, keepdims=True)
    e = jnp.where(valid, jnp.exp(logits - m_loc), 0.0)
    s_loc = jnp.sum(e, axis=1, keepdims=True)
    t_loc = jnp.sum(jnp.where(chosen, logits, 0.0), axis=1, keepdims=True)
    stat[r_me] = jnp.where(lane16 == 0, m_loc, jnp.where(lane16 == 1, s_loc, t_loc))

    def st_copy(o):
        return remote(
            stat.at[r_me], stat.at[r_me], st_send.at[o], st_recv.at[r_me], me.row_group((r_me + o) % 8)
        )

    for o in range(1, 8):
        st_copy(o).start()
    for o in range(1, 8):
        q = (r_me + o) % 8
        remote(stat.at[r_me], stat.at[q], st_send.at[o], st_recv.at[q], me.row_group(q)).wait_recv()
    row_max = stat[0][:, 0:1]
    for q in range(1, 8):
        row_max = jnp.maximum(row_max, stat[q][:, 0:1])
    row_total = jnp.zeros((16, 1), F32)
    target_logit = jnp.zeros((16, 1), F32)
    for q in range(8):
        row_total += stat[q][:, 1:2] * jnp.exp(stat[q][:, 0:1] - row_max)
        target_logit += stat[q][:, 2:3]
    loss = jnp.log(row_total) + row_max - target_logit
    grad = e * (jnp.exp(m_loc - row_max) / row_total) - jnp.where(chosen, 1.0, 0.0)
    hi = loss.astype(BF16).astype(F32)
    mid = (loss - hi).astype(BF16).astype(F32)
    low = loss - hi - mid
    grad = jnp.where(col == VH, hi, grad)
    grad = jnp.where(col == VH + 1, mid, grad)
    grad = jnp.where(col == VH + 2, low, grad)

    def rows_of(b):
        return pl.ds(pl.multiple_of(b * 16, 16), 16)

    gsend[...] = grad.astype(BF16)

    @pl.when(c == d)
    def _():
        gbuf[rows_of(d * 8 + k), :] = gsend[...]

    def ag_copy(q):
        return remote(
            gsend, gbuf.at[rows_of(d * 8 + k)], ag_send.at[q], ag_recv.at[k], me.half_group(q)
        )

    def pf_copy(u, core):
        rows = rows_of(core * 8 + u)
        return remote(gbuf.at[rows], gbuf.at[rows], pf_send.at[u], pf_recv.at[u], me.partner())

    def is_other(q):
        return jnp.logical_or(c != d, q != k)

    for o in range(8):
        q = (k + o) % 8

        @pl.when(is_other(q))
        def _():
            ag_copy(q).start()

    for o in range(8):
        u = (k + 8 - o) % 8

        @pl.when(is_other(u))
        def _():
            remote(
                gsend, gbuf.at[rows_of(c * 8 + u)], ag_send.at[0], ag_recv.at[u], me.partner()
            ).wait_recv()

        pf_copy(u, c).start()
    for u in range(8):
        pf_copy(u, 1 - c).wait_recv()

    g_copy = pltpu.make_async_copy(gbuf, g_out, out_sem.at[2])
    g_copy.start()
    give_hid.wait_recv()
    hid_copy = pltpu.make_async_copy(hid, hid_out, out_sem.at[1])
    hid_copy.start()
    give_emb.wait_recv()
    emb_copy = pltpu.make_async_copy(emb, emb_out, out_sem.at[0])
    emb_copy.start()

    def hg_copy(o):
        q = (g_me + o) % 8
        return remote(hq.at[q], hr.at[g_me], hg_send.at[o], hg_recv.at[g_me], me.group(q))

    def columns(n, carry):
        cols = pl.ds(pl.multiple_of(n * HN, HN), HN)
        hgf[:, cols] = jnp.dot(gbuf[...], wsh[:, cols], preferred_element_type=F32)
        return carry

    lax.fori_loop(0, DM // HN, columns, 0)
    code, scale = quantize(hgf[...].reshape(8, 32, DM))
    hq[:, :, 0:DM] = code
    hq[:, :, DM:] = jnp.broadcast_to(scale, (8, 32, 128)).astype(I32).astype(I16)
    for o in range(1, 8):
        hg_copy(o).start()
    hr[g_me] = hq[g_me]

    tile = gbuf[rows_of(d * 8 + me.p // 2), pl.ds(NC - 128, 128)].astype(F32)
    half = jnp.where(me.p % 2 == 0, tile[0:8, :], tile[8:16, :])
    lane8 = lax.broadcasted_iota(I32, (8, 128), 1)
    here = jnp.logical_and(lane8 >= VH - (NC - 128), lane8 < VH + 3 - (NC - 128))
    value = jnp.sum(jnp.where(here, half, 0.0), axis=1, keepdims=True)
    loss_out[...] = jnp.broadcast_to(value, (8, 128))

    for o in range(1, 8):
        q = (g_me + o) % 8
        remote(hq.at[q], hr.at[q], hg_send.at[o], hg_recv.at[q], me.group(q)).wait_recv()
    total = jnp.zeros((32, DM), F32)
    for q in range(8):
        unit = scale_of(hr[q, :, DM:].astype(I32).astype(F32))[:, 0:1] * (1.0 / TOP)
        total += hr[q, :, 0:DM].astype(I32).astype(F32) * unit
    hg_out[...] = total.astype(BF16)

    give_hid.wait_send()
    give_tok.wait_send()
    give_emb.wait_send()
    emb_copy.wait()
    hid_copy.wait()
    g_copy.wait()

    def drain(j, carry):
        xc_copy(2 * j + 1 - c).wait_send()
        return carry

    lax.fori_loop(0, NJ, drain, 0)
    for o in range(1, 8):
        for part_no in range(NP):
            rs_copy((k + o) % 8, part_no, k).wait_send()
    for o in range(1, 8):
        st_copy(o).wait_send()
    for q in range(8):

        @pl.when(is_other(q))
        def _():
            ag_copy(q).wait_send()

    for q in range(8):
        pf_copy(q, c).wait_send()
    for o in range(1, 8):
        hg_copy(o).wait_send()


def comm_call(tokens, targets, hidden, embed, word):
    any_, vmem = pl.BlockSpec(memory_space=pl.ANY), pl.BlockSpec(memory_space=pltpu.VMEM)
    dma = pltpu.SemaphoreType.DMA
    return pl.pallas_call(
        comm_kernel,
        grid=(1,),
        out_shape=(
            jax.ShapeDtypeStruct((256, NC), BF16),
            jax.ShapeDtypeStruct((2, 128, DM), BF16),
            jax.ShapeDtypeStruct((2, 128, DM), BF16),
            jax.ShapeDtypeStruct((8, 128), I32),
            jax.ShapeDtypeStruct((8, 128), F32),
            jax.ShapeDtypeStruct((32, DM), BF16),
        ),
        in_specs=[
            vmem, vmem, any_, any_, any_,
            pl.BlockSpec((16, DM), lambda i: (2 * MAIN // 16, 0)),
        ],
        out_specs=(any_, any_, any_, vmem, vmem, vmem),
        scratch_shapes=[
            pltpu.VMEM((2, NC + 16, DM), BF16),
            pltpu.VMEM((NC, DM), BF16),
            pltpu.VMEM((2, 128, DM), BF16),
            pltpu.VMEM((2, 128, DM), BF16),
            pltpu.VMEM((NS, 8, 16, CH), F32),
            pltpu.VMEM((NJ, 8, 16, CH), F32),
            pltpu.VMEM((8, 16, NQ), I16),
            pltpu.VMEM((8, 16, NQ), I16),
            pltpu.VMEM((1, 128), I32),
            pltpu.VMEM((16, NC), F32),
            pltpu.VMEM((8, 16, 128), F32),
            pltpu.VMEM((16, NC), BF16),
            pltpu.VMEM((256, NC), BF16),
            pltpu.VMEM((256, DM), F32),
            pltpu.VMEM((8, 32, DM + 128), I16),
            pltpu.VMEM((8, 32, DM + 128), I16),
            dma((2, NJ)),
            dma((2,)),
            dma((4,)),
            dma((4,)),
            dma((NJ,)),
            dma((NJ,)),
            dma((NP, 8)),
            dma((NP, 8)),
            dma((8,)),
            dma((8,)),
            dma((8,)),
            dma((8,)),
            dma((8,)),
            dma((8,)),
            dma((8,)),
            dma((8,)),
            dma((3,)),
        ],
        compiler_params=pltpu.CompilerParams(
            collective_id=0, has_side_effects=True, vmem_limit_bytes=60 * 2**20
        ),
        name="logit_grad",
    )(tokens, targets, hidden, embed, word, word)


RB = 1152


def word_kernel(g_ref, hid_ref, emb_ref, tok_ref, loss_ref, hg_ref, out_ref, loss_out, hg_out):
    i = pl.program_id(0)
    base = lax.axis_index("tensor") * VS + lax.axis_index("dp") * VH + i * RB
    rows = lax.broadcasted_iota(I32, (RB, 128), 0) + base
    tok = tok_ref[...]
    hot = jnp.concatenate(
        [jnp.where(rows == tok[h : h + 1, :], 1.0, 0.0).astype(BF16) for h in range(2)], axis=1
    )
    head = lax.dot_general(
        g_ref[...], hid_ref[...], (((0,), (0,)), ((), ())), preferred_element_type=F32
    )
    out_ref[...] = head + jnp.dot(hot, emb_ref[...], preferred_element_type=F32)

    @pl.when(i == 0)
    def _():
        sub = lax.broadcasted_iota(I32, (8, 128), 0)
        lane = lax.broadcasted_iota(I32, (8, 128), 1)
        row = jnp.sum(jnp.where(sub == lane, loss_ref[...], 0.0), axis=0, keepdims=True)
        loss_out[...] = row[:, 0:8]
        hg_out[...] = hg_ref[...]


def word_call(grad, hid, emb, tok, loss, hg):
    def whole(*shape):
        return pl.BlockSpec(shape, lambda i: (0,) * len(shape))

    return pl.pallas_call(
        word_kernel,
        grid=(pl.cdiv(VH, RB),),
        out_shape=(
            jax.ShapeDtypeStruct((VH, DM), F32),
            jax.ShapeDtypeStruct((1, 8), F32),
            jax.ShapeDtypeStruct((32, DM), BF16),
        ),
        in_specs=[
            pl.BlockSpec((256, RB), lambda i: (0, i)),
            whole(256, DM), whole(256, DM), whole(8, 128), whole(8, 128), whole(32, DM),
        ],
        out_specs=(pl.BlockSpec((RB, DM), lambda i: (i, 0)), whole(1, 8), whole(32, DM)),
        compiler_params=pltpu.CompilerParams(vmem_limit_bytes=60 * 2**20),
        name="word_grad",
    )(grad, hid, emb, tok, loss, hg)


def local(tokens, targets, hidden, embed_grad, word_matrix):
    grad, hid, emb, tok, loss, hg = comm_call(
        tokens.reshape(1, 128), targets.reshape(1, 128), hidden, embed_grad, word_matrix
    )
    word, loss, hg = word_call(
        grad, hid.reshape(256, DM), emb.reshape(256, DM), tok, loss, hg
    )
    return loss.reshape(8), hg, word


def solution(mesh):
    return jax.shard_map(
        local,
        mesh=mesh,
        in_specs=(P("dp"), P("dp"), P("dp", "pipe"), P("dp", "pipe"), P("tensor", "pipe")),
        out_specs=(P(("dp", "pipe")), P(("dp", "tensor"), "pipe"), P(("tensor", "dp"), "pipe")),
        check_vma=False,
    )
```

```python
import functools

import jax
import jax.numpy as jnp
from jax import lax
from jax.experimental import pallas as pl
from jax.experimental.pallas import tpu as pltpu
from jax.sharding import PartitionSpec as P

MESH = pl.DeviceIdType.MESH
BF16, F32, I32, I16 = jnp.bfloat16, jnp.float32, jnp.int32, jnp.int16

DM = 768
VS = 6284
VH = 3142
SH = 6
MAIN = 3136
NC = 3200
CH = 640
NJ = NC // CH
ENDS = (0, 2, 4, NJ)
NP = len(ENDS) - 1
AHEAD = 2
NQ = NC + 128
LAG = 2
HN = 256
SR = 320
NS = 2 * NJ
TOP = 32767.0


class Place:
    def __init__(self):
        self.d = lax.axis_index("dp")
        self.p = lax.axis_index("pipe")
        self.t = lax.axis_index("tensor")
        self.c = self.p % 2
        self.k = self.p // 2

    def chip(self, k):
        return {"pipe": k * 2 + self.c}

    def partner(self):
        return {"pipe": self.k * 2 + (1 - self.c)}

    def group(self, g):
        return {"dp": g // 4, "tensor": g % 4}

    def row_group(self, g):
        return {"tensor": g // 2, "pipe": self.k * 2 + g % 2}

    def half_group(self, q):
        return {"dp": self.c, "pipe": q * 2 + self.d}


LN2_16 = 0.6931471805599453 / 16


def scale_of(code):
    return jnp.exp(code * LN2_16)


def quantize(x):
    top = jnp.maximum(jnp.max(jnp.abs(x), axis=-1, keepdims=True), 1e-30)
    code = jnp.ceil(jnp.log(top) * (1 / LN2_16) + 0.1)
    return jnp.round(x * (TOP / scale_of(code))).astype(I32).astype(I16), code


def comm_kernel(
    tok_ref, tgt_ref, hid_hbm, emb_hbm, w_hbm, tail_ref,
    g_out, hid_out, emb_out, tok_out, loss_out, hg_out,
    wwin, wsh, hid, emb, part, xch, qbuf, rs, tokx, lbuf, stat, gsend, gbuf,
    hgf, hq, hr,
    w_sem, hid_sem, px_send, px_recv, xc_send, xc_recv, rs_send, rs_recv,
    st_send, st_recv, ag_send, ag_recv, pf_send, pf_recv, hg_send, hg_recv,
    out_sem,
):
    me = Place()
    d, c, k = me.d, me.c, me.k
    h = c
    g_me = d * 4 + me.t
    r_me = me.t * 2 + h

    def remote(src, dst, ssem, rsem, to):
        return pltpu.make_async_remote_copy(
            src_ref=src, dst_ref=dst, send_sem=ssem, recv_sem=rsem, device_id=to, device_id_type=MESH
        )

    def w_copy(v, j):
        rows = CH if j < NJ - 1 else MAIN - (NJ - 1) * CH + (16 if v == 0 else 0)
        return pltpu.make_async_copy(
            w_hbm.at[pl.ds(v * MAIN + j * CH, rows)],
            wwin.at[v, pl.ds(j * CH, rows)],
            w_sem.at[v, j],
        )

    own_hid = pltpu.make_async_copy(hid_hbm, hid.at[d], hid_sem.at[0])
    own_hid.start()
    for j in range(AHEAD):
        for v in range(2):
            w_copy(v, j).start()
    own_emb = pltpu.make_async_copy(emb_hbm, emb.at[d], hid_sem.at[1])
    own_emb.start()

    bar = pltpu.get_barrier_semaphore()

    def greet(to):
        pl.semaphore_signal(bar, inc=1, device_id=to, device_id_type=MESH)

    greet(me.partner())
    for o in range(1, 8):
        greet(me.chip((k + o) % 8))
        greet(me.group((g_me + o) % 8))
    for o in range(1, 4):
        greet({"tensor": (me.t + o) % 4, "pipe": k * 2 + 1 - c})

    for q in range(8):
        greet({"dp": 1 - d, "pipe": q * 2 + 1 - c})
    pl.semaphore_wait(bar, 26)

    other = {"dp": 1 - d}
    give_hid = remote(hid.at[d], hid.at[d], px_send.at[0], px_recv.at[0], other)
    give_tok = remote(tok_ref, tokx, px_send.at[2], px_recv.at[2], other)
    give_tok.start()

    row16 = lax.broadcasted_iota(I32, (16, DM), 0)
    tail = jnp.where(row16 < VS - 2 * MAIN, tail_ref[...].astype(F32), 0.0)
    wwin[1, pl.ds(MAIN, 16), :] = tail.astype(BF16)
    for v in range(2):
        wwin[v, pl.ds(MAIN + 16, NC - MAIN), :] = jnp.zeros((NC - MAIN, DM), BF16)
    qbuf[:, :, pl.ds(NC, 128)] = jnp.zeros((8, 16, 128), I16)

    def xc_copy(s):
        return remote(part.at[s], xch.at[s // 2], xc_send.at[s // 2], xc_recv.at[s // 2], me.partner())

    def rs_copy(q, part_no, source):
        first, end = ENDS[part_no] * CH, ENDS[part_no + 1] * CH
        cols = pl.ds(first, (end if part_no < NP - 1 else NQ) - first)
        return remote(
            qbuf.at[q, :, cols], rs.at[source, :, cols], rs_send.at[part_no, q],
            rs_recv.at[part_no, source], me.chip(q),
        )

    def multiply(s):
        v = s % 2
        cols = pl.ds(pl.multiple_of((s // 2) * CH, CH), CH)
        prod = lax.dot_general(
            hid[d], wwin[v, cols, :], (((1,), (1,)), ((), ())), preferred_element_type=F32
        )
        part[s] = prod.reshape(8, 16, CH)

    def finish(j):
        xc_copy(2 * j + c).wait_recv()
        total = part[2 * j + c] + xch[j]
        code, scale = quantize(total)
        qbuf[:, :, pl.ds(pl.multiple_of(j * CH, CH), CH)] = code
        lane = lax.broadcasted_iota(I32, (8, 16, 128), 2)
        kept = qbuf[:, :, pl.ds(NC, 128)].astype(I32)
        kept = jnp.where(lane == j, scale.astype(I32), kept)
        qbuf[:, :, pl.ds(NC, 128)] = kept.astype(I16)
        for part_no in range(NP):

            @pl.when(j == ENDS[part_no + 1] - 1)
            def _():
                for o in range(1, 8):
                    rs_copy((k + o) % 8, part_no, k).start()

    own_hid.wait()
    give_hid.start()

    def step(j, carry):
        for jj in range(NJ):

            @pl.when(j == jj)
            def _():
                w_copy(0, jj).wait()
                w_copy(1, jj).wait()
                if jj + AHEAD < NJ:
                    w_copy(0, jj + AHEAD).start()
                    w_copy(1, jj + AHEAD).start()

        multiply(2 * j + 1 - c)
        xc_copy(2 * j + 1 - c).start()
        multiply(2 * j + c)

        @pl.when(j >= LAG)
        def _():
            finish(j - LAG)

        return carry

    lax.fori_loop(0, NJ, step, 0)

    def finish_step(j, carry):
        finish(j)
        return carry

    lax.fori_loop(NJ - LAG, NJ, finish_step, 0)
    rs[k] = qbuf[k]

    def shift(i, carry):
        rows = pl.multiple_of(i * SR, 64)
        wide = wwin[d, pl.ds(rows, SR + 16), :].astype(F32)
        moved = jnp.where(d == 0, wide[0:SR, :], wide[SH : SH + SR, :])
        wsh[pl.ds(rows, SR), :] = moved.astype(BF16)
        return carry

    lax.fori_loop(0, NC // SR, shift, 0)
    row_l = lax.broadcasted_iota(I32, (NC - MAIN, DM), 0) + MAIN
    end = wsh[pl.ds(MAIN, NC - MAIN), :].astype(F32)
    wsh[pl.ds(MAIN, NC - MAIN), :] = jnp.where(row_l < VH, end, 0.0).astype(BF16)

    lane16 = lax.broadcasted_iota(I32, (16, 128), 1)
    sub16 = lax.broadcasted_iota(I32, (16, 128), 0)
    tgt = jnp.sum(
        jnp.where(lane16 == sub16 + k * 16, tgt_ref[...].astype(F32), 0.0), axis=1, keepdims=True
    ).astype(I32)
    offset = me.t * VS + h * VH
    give_tok.wait_recv()
    sub8 = lax.broadcasted_iota(I32, (8, 128), 0)
    tok_out[...] = jnp.where(sub8 == d, tok_ref[...], tokx[...])

    for o in range(1, 8):
        for part_no in range(NP):
            rs_copy((k + o) % 8, part_no, (k + o) % 8).wait_recv()

    own_emb.wait()
    give_emb = remote(emb.at[d], emb.at[d], px_send.at[3], px_recv.at[3], other)
    give_emb.start()

    units = [scale_of(rs[q, :, NC:NQ].astype(I32).astype(F32)) * (1.0 / TOP) for q in range(8)]
    for j in range(NJ):
        total = jnp.zeros((16, CH), F32)
        for q in range(8):
            total += rs[q, :, j * CH : (j + 1) * CH].astype(I32).astype(F32) * units[q][:, j : j + 1]
        lbuf[:, j * CH : (j + 1) * CH] = total

    logits = pltpu.roll(lbuf[...], (NC - SH * h) % NC, 1)
    col = lax.broadcasted_iota(I32, (16, NC), 1)
    valid = col < VH
    logits = jnp.where(valid, logits, -1e30)
    chosen = jnp.logical_and(col == (tgt - offset), valid)
    m_loc = jnp.max(logits, axis=1, keepdims=True)
    e = jnp.where(valid, jnp.exp(logits - m_loc), 0.0)
    s_loc = jnp.sum(e, axis=1, keepdims=True)
    t_loc = jnp.sum(jnp.where(chosen, logits, 0.0), axis=1, keepdims=True)
    stat[r_me] = jnp.where(lane16 == 0, m_loc, jnp.where(lane16 == 1, s_loc, t_loc))

    def st_copy(o):
        return remote(
            stat.at[r_me], stat.at[r_me], st_send.at[o], st_recv.at[r_me], me.row_group((r_me + o) % 8)
        )

    for o in range(1, 8):
        st_copy(o).start()
    for o in range(1, 8):
        q = (r_me + o) % 8
        remote(stat.at[r_me], stat.at[q], st_send.at[o], st_recv.at[q], me.row_group(q)).wait_recv()
    row_max = stat[0][:, 0:1]
    for q in range(1, 8):
        row_max = jnp.maximum(row_max, stat[q][:, 0:1])
    row_total = jnp.zeros((16, 1), F32)
    target_logit = jnp.zeros((16, 1), F32)
    for q in range(8):
        row_total += stat[q][:, 1:2] * jnp.exp(stat[q][:, 0:1] - row_max)
        target_logit += stat[q][:, 2:3]
    loss = jnp.log(row_total) + row_max - target_logit
    grad = e * (jnp.exp(m_loc - row_max) / row_total) - jnp.where(chosen, 1.0, 0.0)
    hi = loss.astype(BF16).astype(F32)
    mid = (loss - hi).astype(BF16).astype(F32)
    low = loss - hi - mid
    grad = jnp.where(col == VH, hi, grad)
    grad = jnp.where(col == VH + 1, mid, grad)
    grad = jnp.where(col == VH + 2, low, grad)

    def rows_of(b):
        return pl.ds(pl.multiple_of(b * 16, 16), 16)

    gsend[...] = grad.astype(BF16)

    @pl.when(c == d)
    def _():
        gbuf[rows_of(d * 8 + k), :] = gsend[...]

    def ag_copy(q):
        return remote(
            gsend, gbuf.at[rows_of(d * 8 + k)], ag_send.at[q], ag_recv.at[k], me.half_group(q)
        )

    def pf_copy(u, core):
        rows = rows_of(core * 8 + u)
        return remote(gbuf.at[rows], gbuf.at[rows], pf_send.at[u], pf_recv.at[u], me.partner())

    def is_other(q):
        return jnp.logical_or(c != d, q != k)

    for o in range(8):
        q = (k + o) % 8

        @pl.when(is_other(q))
        def _():
            ag_copy(q).start()

    for o in range(8):
        u = (k + 8 - o) % 8

        @pl.when(is_other(u))
        def _():
            remote(
                gsend, gbuf.at[rows_of(c * 8 + u)], ag_send.at[0], ag_recv.at[u], me.partner()
            ).wait_recv()

        pf_copy(u, c).start()
    for u in range(8):
        pf_copy(u, 1 - c).wait_recv()

    g_copy = pltpu.make_async_copy(gbuf, g_out, out_sem.at[2])
    g_copy.start()
    give_hid.wait_recv()
    hid_copy = pltpu.make_async_copy(hid, hid_out, out_sem.at[1])
    hid_copy.start()
    give_emb.wait_recv()
    emb_copy = pltpu.make_async_copy(emb, emb_out, out_sem.at[0])
    emb_copy.start()

    def hg_copy(q):
        return remote(hq.at[q], hr.at[g_me], hg_send.at[q], hg_recv.at[g_me], me.group(q))

    def hidden_rows(e):
        rows = pl.ds(pl.multiple_of(e * 128, 128), 128)

        def columns(n, carry):
            cols = pl.ds(pl.multiple_of(n * HN, HN), HN)
            hgf[:, cols] = jnp.dot(gbuf[rows, :], wsh[:, cols], preferred_element_type=F32)
            return carry

        lax.fori_loop(0, DM // HN, columns, 0)
        code, scale = quantize(hgf[...].reshape(4, 32, DM))
        four = pl.ds(e * 4, 4)
        hq[four, :, 0:DM] = code
        hq[four, :, DM:] = jnp.broadcast_to(scale, (4, 32, 128)).astype(I32).astype(I16)

    far = [(1 - d) * 4 + (me.t + o) % 4 for o in range(4)]
    near = [d * 4 + (me.t + o) % 4 for o in range(1, 4)]
    hidden_rows(1 - d)
    for q in far:
        hg_copy(q).start()
    hidden_rows(d)
    for q in near:
        hg_copy(q).start()
    hr[g_me] = hq[g_me]

    tile = gbuf[rows_of(d * 8 + me.p // 2), pl.ds(NC - 128, 128)].astype(F32)
    half = jnp.where(me.p % 2 == 0, tile[0:8, :], tile[8:16, :])
    lane8 = lax.broadcasted_iota(I32, (8, 128), 1)
    here = jnp.logical_and(lane8 >= VH - (NC - 128), lane8 < VH + 3 - (NC - 128))
    value = jnp.sum(jnp.where(here, half, 0.0), axis=1, keepdims=True)
    loss_out[...] = jnp.broadcast_to(value, (8, 128))

    for q in far + near:
        remote(hq.at[q], hr.at[q], hg_send.at[q], hg_recv.at[q], me.group(q)).wait_recv()
    total = jnp.zeros((32, DM), F32)
    for q in range(8):
        unit = scale_of(hr[q, :, DM:].astype(I32).astype(F32))[:, 0:1] * (1.0 / TOP)
        total += hr[q, :, 0:DM].astype(I32).astype(F32) * unit
    hg_out[...] = total.astype(BF16)

    give_hid.wait_send()
    give_tok.wait_send()
    give_emb.wait_send()
    emb_copy.wait()
    hid_copy.wait()
    g_copy.wait()

    def drain(j, carry):
        xc_copy(2 * j + 1 - c).wait_send()
        return carry

    lax.fori_loop(0, NJ, drain, 0)
    for o in range(1, 8):
        for part_no in range(NP):
            rs_copy((k + o) % 8, part_no, k).wait_send()
    for o in range(1, 8):
        st_copy(o).wait_send()
    for q in range(8):

        @pl.when(is_other(q))
        def _():
            ag_copy(q).wait_send()

    for q in range(8):
        pf_copy(q, c).wait_send()
    for q in far + near:
        hg_copy(q).wait_send()


def comm_call(tokens, targets, hidden, embed, word):
    any_, vmem = pl.BlockSpec(memory_space=pl.ANY), pl.BlockSpec(memory_space=pltpu.VMEM)
    dma = pltpu.SemaphoreType.DMA
    return pl.pallas_call(
        comm_kernel,
        grid=(1,),
        out_shape=(
            jax.ShapeDtypeStruct((256, NC), BF16),
            jax.ShapeDtypeStruct((2, 128, DM), BF16),
            jax.ShapeDtypeStruct((2, 128, DM), BF16),
            jax.ShapeDtypeStruct((8, 128), I32),
            jax.ShapeDtypeStruct((8, 128), F32),
            jax.ShapeDtypeStruct((32, DM), BF16),
        ),
        in_specs=[
            vmem, vmem, any_, any_, any_,
            pl.BlockSpec((16, DM), lambda i: (2 * MAIN // 16, 0)),
        ],
        out_specs=(any_, any_, any_, vmem, vmem, vmem),
        scratch_shapes=[
            pltpu.VMEM((2, NC + 16, DM), BF16),
            pltpu.VMEM((NC, DM), BF16),
            pltpu.VMEM((2, 128, DM), BF16),
            pltpu.VMEM((2, 128, DM), BF16),
            pltpu.VMEM((NS, 8, 16, CH), F32),
            pltpu.VMEM((NJ, 8, 16, CH), F32),
            pltpu.VMEM((8, 16, NQ), I16),
            pltpu.VMEM((8, 16, NQ), I16),
            pltpu.VMEM((1, 128), I32),
            pltpu.VMEM((16, NC), F32),
            pltpu.VMEM((8, 16, 128), F32),
            pltpu.VMEM((16, NC), BF16),
            pltpu.VMEM((256, NC), BF16),
            pltpu.VMEM((128, DM), F32),
            pltpu.VMEM((8, 32, DM + 128), I16),
            pltpu.VMEM((8, 32, DM + 128), I16),
            dma((2, NJ)),
            dma((2,)),
            dma((4,)),
            dma((4,)),
            dma((NJ,)),
            dma((NJ,)),
            dma((NP, 8)),
            dma((NP, 8)),
            dma((8,)),
            dma((8,)),
            dma((8,)),
            dma((8,)),
            dma((8,)),
            dma((8,)),
            dma((8,)),
            dma((8,)),
            dma((3,)),
        ],
        compiler_params=pltpu.CompilerParams(
            collective_id=0, has_side_effects=True, vmem_limit_bytes=60 * 2**20
        ),
        name="logit_grad",
    )(tokens, targets, hidden, embed, word, word)


RB = 1152


def word_kernel(g_ref, hid_ref, emb_ref, tok_ref, loss_ref, hg_ref, out_ref, loss_out, hg_out):
    i = pl.program_id(0)
    base = lax.axis_index("tensor") * VS + lax.axis_index("dp") * VH + i * RB
    rows = lax.broadcasted_iota(I32, (RB, 128), 0) + base
    tok = tok_ref[...]
    hot = jnp.concatenate(
        [jnp.where(rows == tok[h : h + 1, :], 1.0, 0.0).astype(BF16) for h in range(2)], axis=1
    )
    head = lax.dot_general(
        g_ref[...], hid_ref[...], (((0,), (0,)), ((), ())), preferred_element_type=F32
    )
    out_ref[...] = head + jnp.dot(hot, emb_ref[...], preferred_element_type=F32)

    @pl.when(i == 0)
    def _():
        sub = lax.broadcasted_iota(I32, (8, 128), 0)
        lane = lax.broadcasted_iota(I32, (8, 128), 1)
        row = jnp.sum(jnp.where(sub == lane, loss_ref[...], 0.0), axis=0, keepdims=True)
        loss_out[...] = row[:, 0:8]
        hg_out[...] = hg_ref[...]


def word_call(grad, hid, emb, tok, loss, hg):
    def whole(*shape):
        return pl.BlockSpec(shape, lambda i: (0,) * len(shape))

    return pl.pallas_call(
        word_kernel,
        grid=(pl.cdiv(VH, RB),),
        out_shape=(
            jax.ShapeDtypeStruct((VH, DM), F32),
            jax.ShapeDtypeStruct((1, 8), F32),
            jax.ShapeDtypeStruct((32, DM), BF16),
        ),
        in_specs=[
            pl.BlockSpec((256, RB), lambda i: (0, i)),
            whole(256, DM), whole(256, DM), whole(8, 128), whole(8, 128), whole(32, DM),
        ],
        out_specs=(pl.BlockSpec((RB, DM), lambda i: (i, 0)), whole(1, 8), whole(32, DM)),
        compiler_params=pltpu.CompilerParams(vmem_limit_bytes=60 * 2**20),
        name="word_grad",
    )(grad, hid, emb, tok, loss, hg)


def local(tokens, targets, hidden, embed_grad, word_matrix):
    grad, hid, emb, tok, loss, hg = comm_call(
        tokens.reshape(1, 128), targets.reshape(1, 128), hidden, embed_grad, word_matrix
    )
    word, loss, hg = word_call(
        grad, hid.reshape(256, DM), emb.reshape(256, DM), tok, loss, hg
    )
    return loss.reshape(8), hg, word


def solution(mesh):
    return jax.shard_map(
        local,
        mesh=mesh,
        in_specs=(P("dp"), P("dp"), P("dp", "pipe"), P("dp", "pipe"), P("tensor", "pipe")),
        out_specs=(P(("dp", "pipe")), P(("dp", "tensor"), "pipe"), P(("tensor", "dp"), "pipe")),
        check_vma=False,
    )
```
